32 devices in a mesh: sen: 8 (over z, core), par: 4 (over y, x).
Axes of the slice: x: 2, y: 2, z: 4, core: 2. Of those that a mesh axis runs over, the one named last changes fastest.
Arguments:
- freq_blocks: bfloat16 [2, 211, 512, 2048], P(None, None, 'sen', 'par'), may hold values from -0.1875 to 0.1875
- noise_index: int32 [512, 210], P('sen'), may hold values from 0 to 63
- noise_levels: float32 [64], replicated, may hold values from 0.25 to 4
- prior: float32 [2048], P('par'), may hold values from 0.3 to 3
- right_side: float32 [8, 210, 2048], P(None, None, 'par'), may hold values from -1.8 to 1.8
Outputs:
- solution: float32 [8, 210, 2048], P(None, None, 'par')
- residual: float32 [8, 210, 2048], P(None, None, 'par')
The draws below stay inside these ranges and needn't reach their ends.
All inputs are finite; a program needn't handle non-finite values.
Results may differ from the reference program's by a relative error of at most 0.0061.
Values may be sent and summed in bfloat16 or wider, within the bound.
A program may use at most 192 MiB of HBM per device.

```python
import math
import jax
import jax.numpy as jnp
from jax import lax

SENSORS = 512
PARAMS = 2048
STEPS = 210
LEVELS = 64
SOURCES = 8
ITERS = 2
PADDED = 420
FREQS = 211


def draw_right_side(key, part):
    key_noise = jax.random.fold_in(jax.random.fold_in(key, 7), 0)
    ramp_scale = 1.0 + 2.0 * jnp.arange(PARAMS, dtype=jnp.float32) / jnp.float32(PARAMS - 1)
    values = 0.1 * jnp.clip(jax.random.normal(key_noise, (SOURCES, STEPS, PARAMS), jnp.float32), -6.0, 6.0)
    return (values * ramp_scale[None, None, :]).astype(jnp.float32)


def plant(drawn, key, smallest, high):
    place = [jax.random.randint(jax.random.fold_in(key, axis), (), 0, length) for axis, length in enumerate(drawn.shape)]
    longest = drawn.shape.index(max(drawn.shape))
    next_to = place[:longest] + [(place[longest] + 1) % drawn.shape[longest]] + place[longest + 1:]
    return drawn.at[tuple(place)].set(smallest).at[tuple(next_to)].set(high)


def strengthened(array, key, source, target, shards_of, factor):
    def block_of(axis_at):
        return (jnp.arange(array.shape[axis_at]) // (array.shape[axis_at] // shards_of)).reshape((-1,) + (1,) * (array.ndim - 1 - axis_at))

    near = jax.random.permutation(key, shards_of)[block_of(target)]
    other_side = (block_of(target) + shards_of // 2) % shards_of
    return jnp.where((block_of(source) == near) | (block_of(source) == other_side), factor * array, array)


def levels(stream_key, shape, cuts, smallest, high):
    def one(dim, blocks):
        heights = jax.random.uniform(jax.random.fold_in(jax.random.fold_in(stream_key, 6), dim), (blocks,), jnp.float32, smallest / len(cuts), high / len(cuts))
        return jnp.repeat(jnp.exp(heights), shape[dim] // blocks).reshape((-1,) + (1,) * (len(shape) - dim - 1))

    loudness = one(*cuts[0])
    for cut in cuts[1:]:
        loudness = loudness * one(*cut)
    return loudness


def gaussian_with(own_key, extent, width, bound, pieces, heavy, held_as=jnp.bfloat16):
    array = width * jax.random.normal(own_key, extent, jnp.float32)
    if pieces:
        array = array * levels(own_key, extent, pieces, -0.22, 0.18)
    return jnp.clip(strengthened(array, jax.random.fold_in(own_key, 3), *heavy), -bound, bound).astype(held_as)


def setup_inputs(seed: int = 0) -> dict:
    splits = jax.random.split(jax.random.key(seed), 6)
    freq_blocks = gaussian_with(splits[0], (2, FREQS, SENSORS, PARAMS), PARAMS ** -0.5, 0.1875, ((2, 8), (3, 4)), (2, 3, 8, 2.0))
    noise_index = plant(jax.random.randint(splits[1], (SENSORS, STEPS), 0, LEVELS), jax.random.fold_in(splits[1], 1), 0, LEVELS - 1).astype(jnp.int32)
    noise_levels = jnp.clip(jnp.exp(jax.random.uniform(splits[2], (LEVELS,), jnp.float32, math.log(0.25), math.log(4.0))), 0.25, 4.0)
    prior = jnp.clip(jnp.exp(math.log(3.0) - 2.3025851 * jax.random.uniform(splits[3], (PARAMS,), jnp.float32) ** levels(splits[3], (PARAMS,), ((0, 4),), -0.2, 0.2)), 0.3, 3.0)
    right_side = draw_right_side(jax.random.fold_in(splits[5], 71), 0)
    return {"freq_blocks": freq_blocks, "noise_index": noise_index, "noise_levels": noise_levels, "prior": prior, "right_side": right_side}


def make_tables(time_length, freq_count, period):
    time_index = jnp.arange(time_length, dtype=jnp.int32)
    freq_index = jnp.arange(freq_count, dtype=jnp.int32)
    phases = (freq_index[:, None] * time_index[None, :]) % period
    angles = phases.astype(jnp.float32) * jnp.float32(2.0 * math.pi / period)
    end_mask = (freq_index == 0) | (freq_index == period // 2)
    inverse_scale = jnp.where(end_mask, jnp.float32(1.0), jnp.float32(2.0)) / jnp.float32(period)
    return jnp.cos(angles), jnp.sin(angles), inverse_scale


def reference(freq_blocks, noise_index, noise_levels, prior, right_side):
    cosine_table, sine_table, inverse_scale = make_tables(STEPS, FREQS, PADDED)
    weights = noise_levels[noise_index]
    highest = lax.Precision.HIGHEST

    def forward_block(index, spec_real, spec_imag):
        block = lax.dynamic_index_in_dim(freq_blocks, index, 1, keepdims=False)
        real_in = lax.dynamic_index_in_dim(spec_real, index, 0, keepdims=False)
        imag_in = lax.dynamic_index_in_dim(spec_imag, index, 0, keepdims=False)
        first_re = jnp.dot(block[0], real_in.T, preferred_element_type=jnp.float32)
        first_im = jnp.dot(block[1], real_in.T, preferred_element_type=jnp.float32)
        second_re = jnp.dot(block[0], imag_in.T, preferred_element_type=jnp.float32)
        second_im = jnp.dot(block[1], imag_in.T, preferred_element_type=jnp.float32)
        return jnp.stack([first_re - second_im, second_re + first_im])

    def adjoint_block(index, back_real, back_imag):
        block = lax.dynamic_index_in_dim(freq_blocks, index, 1, keepdims=False)
        real_in = lax.dynamic_index_in_dim(back_real, index, 0, keepdims=False)
        imag_in = lax.dynamic_index_in_dim(back_imag, index, 0, keepdims=False)
        grad_real = jnp.dot(real_in.T, block[0], preferred_element_type=jnp.float32) + jnp.dot(imag_in.T, block[1], preferred_element_type=jnp.float32)
        grad_imag = jnp.dot(imag_in.T, block[0], preferred_element_type=jnp.float32) - jnp.dot(real_in.T, block[1], preferred_element_type=jnp.float32)
        return jnp.stack([grad_real, grad_imag])

    freq_ids = jnp.arange(FREQS, dtype=jnp.int32)

    def hessian(direction):
        spec_real = jnp.einsum('btj,kt->kbj', direction, cosine_table, precision=highest).astype(jnp.bfloat16)
        spec_imag = (-jnp.einsum('btj,kt->kbj', direction, sine_table, precision=highest)).astype(jnp.bfloat16)
        spectrum = lax.map(lambda index: forward_block(index, spec_real, spec_imag), freq_ids)
        spectrum = jnp.moveaxis(spectrum, 1, 0) * inverse_scale[None, :, None, None]
        predicted = jnp.einsum('ksb,kt->sbt', spectrum[0], cosine_table, precision=highest) - jnp.einsum('ksb,kt->sbt', spectrum[1], sine_table, precision=highest)
        weighted = weights[:, None, :] * predicted
        back_real = (jnp.einsum('sbt,kt->ksb', weighted, cosine_table, precision=highest) * inverse_scale[:, None, None]).astype(jnp.bfloat16)
        back_imag = (-jnp.einsum('sbt,kt->ksb', weighted, sine_table, precision=highest) * inverse_scale[:, None, None]).astype(jnp.bfloat16)
        gradient = lax.map(lambda index: adjoint_block(index, back_real, back_imag), freq_ids)
        curved = jnp.einsum('kbj,kt->btj', gradient[:, 0], cosine_table, precision=highest) - jnp.einsum('kbj,kt->btj', gradient[:, 1], sine_table, precision=highest)
        return curved + prior[None, None, :] * direction

    solution = jnp.zeros_like(right_side)
    residual = right_side
    direction = right_side
    current = jnp.sum(residual * residual, axis=(1, 2))
    for iteration in range(ITERS):
        curved = hessian(direction)
        step_size = current / jnp.sum(direction * curved, axis=(1, 2))
        solution = solution + step_size[:, None, None] * direction
        residual = residual - step_size[:, None, None] * curved
        fresh = jnp.sum(residual * residual, axis=(1, 2))
        direction = residual + (fresh / current)[:, None, None] * direction
        current = fresh
    return solution, residual
```

```python
import functools
import math

import jax
import jax.numpy as jnp
import numpy as np
from jax import lax
from jax.experimental import pallas as pl
from jax.experimental.pallas import tpu as pltpu
from jax.sharding import PartitionSpec as P

ITERS = 2
CHUNKS = 8
LANES = 128
VMEM_BYTES = 58 * 2**20
F32 = jnp.float32
BF16 = jnp.bfloat16
MESH = pl.DeviceIdType.MESH


def tables(steps, freqs):
    period = 2 * steps
    t = np.arange(steps)
    k = np.arange(freqs)
    angle = (k[:, None] * t[None, :] % period) * (2.0 * math.pi / period)
    cos, sin = np.cos(angle), np.sin(angle)
    scale = np.where((k == 0) | (k == period // 2), 1.0, 2.0)[:, None] / period
    rows = lambda a, b: np.stack([a, b], axis=1).reshape(2 * freqs, steps)
    analyse = rows(cos, -sin)
    first = rows(scale * cos, -scale * sin)
    second = rows(-scale * sin, -scale * cos)
    return analyse, first, second


def halves(table):
    high = np.asarray(table, np.float32).astype(jnp.bfloat16)
    low = (np.asarray(table, np.float64) - high.astype(np.float64)).astype(jnp.bfloat16)
    return high, low


def wide(table_high, table_low, x):
    high = x.astype(BF16)
    low = (x - high.astype(F32)).astype(BF16)
    dot = functools.partial(jnp.dot, preferred_element_type=F32)
    return dot(table_high, high) + (dot(table_high, low) + dot(table_low, high))


def chunk_list(freqs):
    edges = [freqs * i // CHUNKS for i in range(CHUNKS + 1)]
    return [(a, b) for a, b in zip(edges[:-1], edges[1:]) if b > a]


def start_copies(blocks, held, sems, chunks):
    copies = []
    for i, (a, b) in enumerate(chunks):
        copy = pltpu.make_async_copy(blocks.at[:, a:b], held.at[:, a:b], sems.at[i])
        copy.start()
        copies.append(copy)
    return copies


def forward_kernel(chunks, pack, ah, al, fh, fl, sh, sl, field, blocks, out, held, spec, prod, sems):
    copies = start_copies(blocks, held, sems, chunks)
    sources = field.shape[0]
    rows = ah.shape[0]
    sensors = held.shape[2]
    for b in range(sources):
        for j in range(spec.shape[0]):
            x = field[b, :, j * LANES : (j + 1) * LANES]
            spec[j, pl.ds(b, rows, stride=sources), :] = wide(ah[...], al[...], x)

    def one(k, _):
        at = pl.ds(pl.multiple_of(k * 2 * sources, 2 * sources), 2 * sources)
        lhs = jnp.concatenate([spec[j, at, :].astype(BF16) for j in range(spec.shape[0])], axis=1)
        rhs = jnp.concatenate([held[0, k], held[1, k]], axis=0)
        prod[at, : 2 * sensors] = lax.dot_general(
            lhs, rhs, (((1,), (1,)), ((), ())), preferred_element_type=F32
        )
        return 0

    for copy, (a, b) in zip(copies, chunks):
        copy.wait()
        lax.fori_loop(a, b, one, 0, unroll=4)
    groups = sources // pack
    for p in range(groups):
        parts = []
        for i in range(pack):
            x = prod[pl.ds(p + i * groups, rows, stride=sources), :]
            parts.append(
                wide(fh[...], fl[...], x[:, :sensors])
                + wide(sh[...], sl[...], x[:, sensors : 2 * sensors])
            )
        out[p] = jnp.concatenate(parts, axis=1).astype(out.dtype)


def adjoint_kernel(
    chunks, pack, fh, fl, sh, sl, ih, il, pred, weights, blocks, out, held, back, grad, sems
):
    copies = start_copies(blocks, held, sems, chunks)
    sources = out.shape[0]
    rows = fh.shape[0]
    sensors = held.shape[2]
    groups = sources // pack
    for p in range(groups):
        weighted = weights[...] * pred[p].astype(F32)
        one_part = wide(fh[...], fl[...], weighted)
        two_part = wide(sh[...], sl[...], weighted)
        for i in range(pack):
            lanes = slice(i * sensors, (i + 1) * sensors)
            row = [one_part[:, lanes], two_part[:, lanes]]
            if 2 * sensors < LANES:
                row.append(jnp.zeros((rows, LANES - 2 * sensors), F32))
            back[pl.ds(p + i * groups, rows, stride=sources), :] = jnp.concatenate(row, axis=1)

    def one(k, _):
        at = pl.ds(pl.multiple_of(k * 2 * sources, 2 * sources), 2 * sources)
        lhs = back[at, : 2 * sensors].astype(BF16)
        rhs = jnp.concatenate([held[0, k], held[1, k]], axis=0)
        made = jnp.dot(lhs, rhs, preferred_element_type=F32)
        for j in range(grad.shape[0]):
            grad[j, at, :] = made[:, j * LANES : (j + 1) * LANES]
        return 0

    for copy, (a, b) in zip(copies, chunks):
        copy.wait()
        lax.fori_loop(a, b, one, 0, unroll=4)
    for b in range(sources):
        for j in range(grad.shape[0]):
            x = grad[j, pl.ds(b, rows, stride=sources), :]
            out[b, :, j * LANES : (j + 1) * LANES] = wide(ih[...], il[...], x).astype(out.dtype)


def forward(consts, blocks, field):
    (ah, al), (fh, fl), (sh, sl) = consts
    _, freqs, sensors, params = blocks.shape
    sources, steps, _ = field.shape
    pack = max(1, min(sources, 128 // sensors))
    chunks = chunk_list(freqs)
    vm = pl.BlockSpec(memory_space=pltpu.VMEM)
    return pl.pallas_call(
        functools.partial(forward_kernel, chunks, pack),
        out_shape=jax.ShapeDtypeStruct((sources // pack, steps, pack * sensors), F32),
        in_specs=[vm] * 7 + [pl.BlockSpec(memory_space=pl.ANY)],
        out_specs=vm,
        scratch_shapes=[
            pltpu.VMEM(blocks.shape, BF16),
            pltpu.VMEM((params // LANES, 2 * freqs * sources, LANES), F32),
            pltpu.VMEM((2 * freqs * sources, max(LANES, 2 * sensors)), F32),
            pltpu.SemaphoreType.DMA((len(chunks),)),
        ],
        compiler_params=pltpu.CompilerParams(vmem_limit_bytes=VMEM_BYTES),
        name="forward",
    )(ah, al, fh.T, fl.T, sh.T, sl.T, field, blocks)


def adjoint(consts, blocks, pred, weights, sources):
    (ah, al), (fh, fl), (sh, sl) = consts
    _, freqs, sensors, params = blocks.shape
    steps = pred.shape[1]
    pack = sources // pred.shape[0]
    chunks = chunk_list(freqs)
    vm = pl.BlockSpec(memory_space=pltpu.VMEM)
    return pl.pallas_call(
        functools.partial(adjoint_kernel, chunks, pack),
        out_shape=jax.ShapeDtypeStruct((sources, steps, params), F32),
        in_specs=[vm] * 8 + [pl.BlockSpec(memory_space=pl.ANY)],
        out_specs=vm,
        scratch_shapes=[
            pltpu.VMEM(blocks.shape, BF16),
            pltpu.VMEM((2 * freqs * sources, max(LANES, 2 * sensors)), F32),
            pltpu.VMEM((params // LANES, 2 * freqs * sources, LANES), F32),
            pltpu.SemaphoreType.DMA((len(chunks),)),
        ],
        compiler_params=pltpu.CompilerParams(vmem_limit_bytes=VMEM_BYTES),
        name="adjoint",
    )(fh, fl, sh, sl, ah.T, al.T, pred, weights, blocks)


def greet(peers):
    barrier = pltpu.get_barrier_semaphore()
    for peer in peers:
        pl.semaphore_signal(barrier, inc=1, device_id=peer, device_id_type=MESH)
    pl.semaphore_wait(barrier, len(peers))


def send(src, dst, send_sem, recv_sem, peer):
    copy = pltpu.make_async_remote_copy(
        src_ref=src,
        dst_ref=dst,
        send_sem=send_sem,
        recv_sem=recv_sem,
        device_id=peer,
        device_id_type=MESH,
    )
    copy.start()
    return copy


def sum_kernel(n, part, out, got, s1, r1, s2, r2):
    me = lax.axis_index("par")
    others = [lax.rem(me + k, n) for k in range(n)]
    greet([{"par": o} for o in others[1:]])
    first = [
        send(part.at[others[k]], got.at[k], s1.at[k], r1.at[k], {"par": others[k]})
        for k in range(1, n)
    ]
    for copy in first:
        copy.wait_recv()
    total = part[me]
    for k in range(1, n):
        total = total + got[k]
    out[me] = total
    second = [
        send(out.at[me], out.at[me], s2.at[k], r2.at[k], {"par": others[k]}) for k in range(1, n)
    ]
    for copy in first:
        copy.wait_send()
    for copy in second:
        copy.wait()


def sum_over_par(part):
    n = lax.axis_size("par")
    if part.shape[0] != n or n == 1:
        return lax.psum(part, "par")
    vm = pl.BlockSpec(memory_space=pltpu.VMEM)
    return pl.pallas_call(
        functools.partial(sum_kernel, n),
        out_shape=jax.ShapeDtypeStruct(part.shape, part.dtype),
        in_specs=[vm],
        out_specs=vm,
        scratch_shapes=[pltpu.VMEM(part.shape, part.dtype)] + [pltpu.SemaphoreType.DMA((n,))] * 4,
        compiler_params=pltpu.CompilerParams(
            collective_id=0, has_side_effects=True, vmem_limit_bytes=16 * 2**20
        ),
        name="sum_par",
    )(part)


def total_of(x):
    return jnp.sum(jnp.sum(x, axis=0, keepdims=True), axis=1, keepdims=True)


def update_kernel(
    n, npar, part, direction, residual, prior, out, scalars,
    core_got, staged, z_got, own, d_own, r_own, small, small_got,
    ls, s1, r1, s2, r2, s3, r3, s4, r4, s5, r5, s6, r6, s7, r7,
):
    me = lax.axis_index("sen")
    nz = n // 2
    z, c = me // 2, lax.rem(me, 2)
    sibling = {"sen": 2 * z + 1 - c}
    mine = lax.axis_index("par")
    par_peers = [{"par": lax.rem(mine + k, npar)} for k in range(1, npar)]
    sen_peers = [{"sen": lax.rem(me + k, n)} for k in range(1, n)]
    up = [lax.rem(z + k, nz) for k in range(nz)]
    down = [lax.rem(z + nz - k, nz) for k in range(nz)]
    loads = [
        pltpu.make_async_copy(direction.at[me], d_own, ls.at[0]),
        pltpu.make_async_copy(residual.at[me], r_own, ls.at[1]),
    ]
    for load in loads:
        load.start()
    greet(sen_peers + par_peers)
    order = [k for k in range(1, nz)] + [0]
    core = {}
    for k in order:
        core[k] = send(part.at[2 * up[k] + 1 - c], core_got.at[k], s1.at[k], r1.at[k], sibling)
    along_z = []
    for k in order:
        core[k].wait_recv()
        summed = part[2 * up[k] + c] + core_got[k]
        if k == 0:
            own[...] = summed
        else:
            staged[k] = summed.astype(BF16)
            along_z.append(
                send(staged.at[k], z_got.at[k], s2.at[k], r2.at[k], {"sen": 2 * up[k] + c})
            )
    for copy in along_z:
        copy.wait_recv()
    for load in loads:
        load.wait()
    curved = own[...] + prior[...] * d_own[...]
    for k in range(1, nz):
        curved = curved + z_got[k].astype(F32)
    own[...] = curved
    tile = jnp.zeros(small.shape[1:], F32)
    row = lax.broadcasted_iota(jnp.int32, tile.shape, 0)

    def par_sum(slot, values, ss, rs):
        filled = tile
        for i, value in enumerate(values):
            filled = jnp.where(row == i, value, filled)
        small[slot] = filled
        sent = [
            send(small.at[slot], small_got.at[slot, k], ss.at[k], rs.at[k], peer)
            for k, peer in enumerate(par_peers)
        ]
        for copy in sent:
            copy.wait()
        small_got[slot, npar - 1] = filled
        total = tile
        for i in range(npar):
            total = total + small_got[slot, lax.rem(mine - i - 1 + npar, npar)]
        return [total[i : i + 1, :1] for i in range(len(values))]

    along, before = par_sum(
        0, [total_of(d_own[...] * own[...]), total_of(r_own[...] * r_own[...])], s3, r3
    )
    step = before / along
    rounded = (r_own[...] - step * own[...]).astype(BF16)
    out[me] = rounded
    gather = [
        send(out.at[me], out.at[me], s4.at[k], r4.at[k], {"sen": 2 * up[k] + c})
        for k in range(1, nz)
    ]
    gather.append(send(out.at[me], out.at[me], s5.at[0], r5.at[0], sibling))
    kept = rounded.astype(F32)
    (fresh,) = par_sum(1, [total_of(kept * kept)], s7, r7)
    scalars[me] = jnp.where(row == 0, step, jnp.where(row == 1, fresh / before, tile))
    told = [
        send(scalars.at[me], scalars.at[me], s6.at[k], r6.at[k], peer)
        for k, peer in enumerate(sen_peers)
    ]
    passed = []
    for k in range(1, nz):
        gather[k - 1].wait_recv()
        chunk = 2 * down[k] + c
        passed.append(send(out.at[chunk], out.at[chunk], s5.at[k], r5.at[k], sibling))
    for k in range(1, nz):
        gather[k - 1].wait_send()
    gather[-1].wait()
    for copy in passed + told:
        copy.wait()
    for k in order:
        core[k].wait_send()
    for copy in along_z:
        copy.wait_send()


def update(part, direction, residual, prior):
    n, npar = lax.axis_size("sen"), lax.axis_size("par")
    sources, steps, params = part.shape
    if n != sources or npar == 1:
        curved = lax.psum(part, "sen") + prior[None, None, :] * direction
        sums = jnp.stack([direction * curved, residual * residual])
        along, before = lax.psum(jnp.sum(sums, axis=(2, 3)), "par")
        step = before / along
        after = residual - step[:, None, None] * curved
        fresh = lax.psum(jnp.sum(after * after, axis=(1, 2)), "par")
        return after, step[:, None, None], (fresh / before)[:, None, None]
    nz = n // 2
    vm = pl.BlockSpec(memory_space=pltpu.VMEM)
    anywhere = pl.BlockSpec(memory_space=pl.ANY)
    chunk = (steps, params)
    dma = pltpu.SemaphoreType.DMA
    after, scalars = pl.pallas_call(
        functools.partial(update_kernel, n, npar),
        out_shape=(
            jax.ShapeDtypeStruct((sources, steps, params), BF16),
            jax.ShapeDtypeStruct((sources, 8, LANES), F32),
        ),
        in_specs=[vm, anywhere, anywhere, vm],
        out_specs=(vm, vm),
        scratch_shapes=[
            pltpu.VMEM((nz,) + chunk, F32),
            pltpu.VMEM((nz,) + chunk, BF16),
            pltpu.VMEM((nz,) + chunk, BF16),
            pltpu.VMEM(chunk, F32),
            pltpu.VMEM(chunk, F32),
            pltpu.VMEM(chunk, F32),
            pltpu.VMEM((2, 8, LANES), F32),
            pltpu.VMEM((2, npar, 8, LANES), F32),
            dma((2,)),
        ]
        + [dma((nz,))] * 4
        + [dma((npar,))] * 2
        + [dma((nz,))] * 4
        + [dma((n,))] * 2
        + [dma((npar,))] * 2,
        compiler_params=pltpu.CompilerParams(
            collective_id=1, has_side_effects=True, vmem_limit_bytes=32 * 2**20
        ),
        name="update",
    )(part, direction, residual, prior[None, :])
    return after.astype(F32), scalars[:, 0:1, 0:1], scalars[:, 1:2, 0:1]


def on_device(freq_blocks, noise_index, noise_levels, prior, right_side):
    sources, steps, _ = right_side.shape
    freqs = freq_blocks.shape[1]
    consts = [halves(table) for table in tables(steps, freqs)]
    level_ids = jnp.arange(noise_levels.shape[0], dtype=jnp.int32)
    pack = max(1, min(sources, LANES // freq_blocks.shape[2]))
    index = jnp.tile(noise_index.T, (1, pack))
    weights = jnp.sum(
        jnp.where(index[None] == level_ids[:, None, None], noise_levels[:, None, None], F32(0.0)),
        axis=0,
    )
    solution = None
    residual = right_side
    direction = right_side
    for iteration in range(ITERS):
        pred = sum_over_par(forward(consts, freq_blocks, direction))
        part = adjoint(consts, freq_blocks, pred, weights, sources)
        residual, step, ratio = update(part, direction, residual, prior)
        moved = step * direction
        solution = moved if solution is None else solution + moved
        if iteration + 1 < ITERS:
            direction = residual + ratio * direction
    return (solution, residual)


def solution(mesh):
    placed = (P(None, None, "sen", "par"), P("sen", None), P(), P("par"), P(None, None, "par"))
    return jax.shard_map(
        on_device,
        mesh=mesh,
        in_specs=placed,
        out_specs=(P(None, None, "par"), P(None, None, "par")),
        check_vma=False,
    )
```

```python
import functools
import math

import jax
import jax.numpy as jnp
import numpy as np
from jax import lax
from jax.experimental import pallas as pl
from jax.experimental.pallas import tpu as pltpu
from jax.sharding import PartitionSpec as P

ITERS = 2
CHUNKS = 8
UNROLL = 16
LANES = 128
VMEM_BYTES = 58 * 2**20
F32 = jnp.float32
BF16 = jnp.bfloat16
MESH = pl.DeviceIdType.MESH


def tables(steps, freqs):
    period = 2 * steps
    t = np.arange(steps)
    k = np.arange(freqs)
    angle = (k[:, None] * t[None, :] % period) * (2.0 * math.pi / period)
    cos, sin = np.cos(angle), np.sin(angle)
    scale = np.where((k == 0) | (k == period // 2), 1.0, 2.0)[:, None] / period
    rows = lambda a, b: np.stack([a, b], axis=1).reshape(2 * freqs, steps)
    analyse = rows(cos, -sin)
    first = rows(scale * cos, -scale * sin)
    second = rows(-scale * sin, -scale * cos)
    return analyse, first, second


def halves(table):
    high = np.asarray(table, np.float32).astype(jnp.bfloat16)
    low = (np.asarray(table, np.float64) - high.astype(np.float64)).astype(jnp.bfloat16)
    return high, low


def wide(table_high, table_low, x):
    high = x.astype(BF16)
    low = (x - high.astype(F32)).astype(BF16)
    dot = functools.partial(jnp.dot, preferred_element_type=F32)
    return dot(table_high, high) + (dot(table_high, low) + dot(table_low, high))


def chunk_list(freqs):
    edges = [freqs * i // CHUNKS for i in range(CHUNKS + 1)]
    return [(a, b) for a, b in zip(edges[:-1], edges[1:]) if b > a]


def start_copies(blocks, held, sems, chunks):
    copies = []
    for i, (a, b) in enumerate(chunks):
        copy = pltpu.make_async_copy(blocks.at[:, a:b], held.at[:, a:b], sems.at[i])
        copy.start()
        copies.append(copy)
    return copies


def forward_kernel(chunks, pack, ah, al, fh, fl, sh, sl, field, blocks, out, held, spec, prod, sems):
    copies = start_copies(blocks, held, sems, chunks)
    sources = field.shape[0]
    rows = ah.shape[0]
    sensors = held.shape[2]
    for b in range(sources):
        made = wide(ah[...], al[...], field[b])
        for j in range(spec.shape[0]):
            spec[j, pl.ds(b, rows, stride=sources), :] = made[:, j * LANES : (j + 1) * LANES]

    def one(k, _):
        at = pl.ds(pl.multiple_of(k * 2 * sources, 2 * sources), 2 * sources)
        lhs = jnp.concatenate([spec[j, at, :].astype(BF16) for j in range(spec.shape[0])], axis=1)
        rhs = jnp.concatenate([held[0, k], held[1, k]], axis=0)
        prod[at, : 2 * sensors] = lax.dot_general(
            lhs, rhs, (((1,), (1,)), ((), ())), preferred_element_type=F32
        )
        return 0

    for copy, (a, b) in zip(copies, chunks):
        copy.wait()
        lax.fori_loop(a, b, one, 0, unroll=UNROLL)
    groups = sources // pack
    real, imag = [], []
    for p in range(groups):
        for i in range(pack):
            x = prod[pl.ds(p + i * groups, rows, stride=sources), :]
            real.append(x[:, :sensors])
            imag.append(x[:, sensors : 2 * sensors])
    made = wide(fh[...], fl[...], jnp.concatenate(real, axis=1))
    made = made + wide(sh[...], sl[...], jnp.concatenate(imag, axis=1))
    for p in range(groups):
        out[p] = made[:, p * pack * sensors : (p + 1) * pack * sensors]


def adjoint_kernel(
    chunks, pack, fh, fl, sh, sl, ih, il, pred, weights, blocks, out, held, back, grad, sems
):
    copies = start_copies(blocks, held, sems, chunks)
    sources = out.shape[0]
    rows = fh.shape[0]
    sensors = held.shape[2]
    groups = sources // pack
    weighted = jnp.concatenate([weights[...] * pred[p] for p in range(groups)], axis=1)
    one_part = wide(fh[...], fl[...], weighted)
    two_part = wide(sh[...], sl[...], weighted)
    for p in range(groups):
        for i in range(pack):
            start = (p * pack + i) * sensors
            row = [x[:, start : start + sensors] for x in (one_part, two_part)]
            if 2 * sensors < LANES:
                row.append(jnp.zeros((rows, LANES - 2 * sensors), F32))
            back[pl.ds(p + i * groups, rows, stride=sources), :] = jnp.concatenate(row, axis=1)

    def one(k, _):
        at = pl.ds(pl.multiple_of(k * 2 * sources, 2 * sources), 2 * sources)
        lhs = back[at, : 2 * sensors].astype(BF16)
        rhs = jnp.concatenate([held[0, k], held[1, k]], axis=0)
        made = jnp.dot(lhs, rhs, preferred_element_type=F32)
        for j in range(grad.shape[0]):
            grad[j, at, :] = made[:, j * LANES : (j + 1) * LANES]
        return 0

    for copy, (a, b) in zip(copies, chunks):
        copy.wait()
        lax.fori_loop(a, b, one, 0, unroll=UNROLL)
    for b in range(sources):
        x = jnp.concatenate(
            [grad[j, pl.ds(b, rows, stride=sources), :] for j in range(grad.shape[0])], axis=1
        )
        out[b] = wide(ih[...], il[...], x)


def forward(consts, blocks, field):
    (ah, al), (fh, fl), (sh, sl) = consts
    _, freqs, sensors, params = blocks.shape
    sources, steps, _ = field.shape
    pack = max(1, min(sources, 128 // sensors))
    chunks = chunk_list(freqs)
    vm = pl.BlockSpec(memory_space=pltpu.VMEM)
    return pl.pallas_call(
        functools.partial(forward_kernel, chunks, pack),
        out_shape=jax.ShapeDtypeStruct((sources // pack, steps, pack * sensors), F32),
        in_specs=[vm] * 7 + [pl.BlockSpec(memory_space=pl.ANY)],
        out_specs=vm,
        scratch_shapes=[
            pltpu.VMEM(blocks.shape, BF16),
            pltpu.VMEM((params // LANES, 2 * freqs * sources, LANES), F32),
            pltpu.VMEM((2 * freqs * sources, max(LANES, 2 * sensors)), F32),
            pltpu.SemaphoreType.DMA((len(chunks),)),
        ],
        compiler_params=pltpu.CompilerParams(vmem_limit_bytes=VMEM_BYTES),
        name="forward",
    )(ah, al, fh.T, fl.T, sh.T, sl.T, field, blocks)


def adjoint(consts, blocks, pred, weights, sources):
    (ah, al), (fh, fl), (sh, sl) = consts
    _, freqs, sensors, params = blocks.shape
    steps = pred.shape[1]
    pack = sources // pred.shape[0]
    chunks = chunk_list(freqs)
    vm = pl.BlockSpec(memory_space=pltpu.VMEM)
    return pl.pallas_call(
        functools.partial(adjoint_kernel, chunks, pack),
        out_shape=jax.ShapeDtypeStruct((sources, steps, params), F32),
        in_specs=[vm] * 8 + [pl.BlockSpec(memory_space=pl.ANY)],
        out_specs=vm,
        scratch_shapes=[
            pltpu.VMEM(blocks.shape, BF16),
            pltpu.VMEM((2 * freqs * sources, max(LANES, 2 * sensors)), F32),
            pltpu.VMEM((params // LANES, 2 * freqs * sources, LANES), F32),
            pltpu.SemaphoreType.DMA((len(chunks),)),
        ],
        compiler_params=pltpu.CompilerParams(vmem_limit_bytes=VMEM_BYTES),
        name="adjoint",
    )(fh, fl, sh, sl, ah.T, al.T, pred, weights, blocks)


def greet(peers):
    barrier = pltpu.get_barrier_semaphore()
    for peer in peers:
        pl.semaphore_signal(barrier, inc=1, device_id=peer, device_id_type=MESH)
    pl.semaphore_wait(barrier, len(peers))


def send(src, dst, send_sem, recv_sem, peer):
    copy = pltpu.make_async_remote_copy(
        src_ref=src,
        dst_ref=dst,
        send_sem=send_sem,
        recv_sem=recv_sem,
        device_id=peer,
        device_id_type=MESH,
    )
    copy.start()
    return copy


def sum_kernel(n, part, out, got, s1, r1, s2, r2):
    me = lax.axis_index("par")
    others = [lax.rem(me + k, n) for k in range(n)]
    greet([{"par": o} for o in others[1:]])
    first = [
        send(part.at[others[k]], got.at[k], s1.at[k], r1.at[k], {"par": others[k]})
        for k in range(1, n)
    ]
    for copy in first:
        copy.wait_recv()
    total = part[me]
    for k in range(1, n):
        total = total + got[k]
    out[me] = total
    second = [
        send(out.at[me], out.at[me], s2.at[k], r2.at[k], {"par": others[k]}) for k in range(1, n)
    ]
    for copy in first:
        copy.wait_send()
    for copy in second:
        copy.wait()


def sum_over_par(part):
    n = lax.axis_size("par")
    if part.shape[0] != n or n == 1:
        return lax.psum(part, "par")
    vm = pl.BlockSpec(memory_space=pltpu.VMEM)
    return pl.pallas_call(
        functools.partial(sum_kernel, n),
        out_shape=jax.ShapeDtypeStruct(part.shape, part.dtype),
        in_specs=[vm],
        out_specs=vm,
        scratch_shapes=[pltpu.VMEM(part.shape, part.dtype)] + [pltpu.SemaphoreType.DMA((n,))] * 4,
        compiler_params=pltpu.CompilerParams(
            collective_id=0, has_side_effects=True, vmem_limit_bytes=16 * 2**20
        ),
        name="sum_par",
    )(part)


def total_of(x):
    return jnp.sum(jnp.sum(x, axis=0, keepdims=True), axis=1, keepdims=True)


def update_kernel(
    n, npar, part, direction, residual, prior, out, scalars,
    core_got, staged, z_got, own, d_own, r_own, small, small_got,
    ls, s1, r1, s2, r2, s3, r3, s4, r4, s5, r5, s6, r6, s7, r7,
):
    me = lax.axis_index("sen")
    nz = n // 2
    z, c = me // 2, lax.rem(me, 2)
    sibling = {"sen": 2 * z + 1 - c}
    mine = lax.axis_index("par")
    par_peers = [{"par": lax.rem(mine + k, npar)} for k in range(1, npar)]
    sen_peers = [{"sen": lax.rem(me + k, n)} for k in range(1, n)]
    up = [lax.rem(z + k, nz) for k in range(nz)]
    down = [lax.rem(z + nz - k, nz) for k in range(nz)]
    loads = [
        pltpu.make_async_copy(direction.at[me], d_own, ls.at[0]),
        pltpu.make_async_copy(residual.at[me], r_own, ls.at[1]),
    ]
    for load in loads:
        load.start()
    greet(sen_peers + par_peers)
    order = [k for k in range(1, nz)] + [0]
    core = {}
    for k in order:
        core[k] = send(part.at[2 * up[k] + 1 - c], core_got.at[k], s1.at[k], r1.at[k], sibling)
    along_z = []
    for k in order:
        core[k].wait_recv()
        summed = part[2 * up[k] + c] + core_got[k]
        if k == 0:
            own[...] = summed
        else:
            staged[k] = summed.astype(BF16)
            along_z.append(
                send(staged.at[k], z_got.at[k], s2.at[k], r2.at[k], {"sen": 2 * up[k] + c})
            )
    for copy in along_z:
        copy.wait_recv()
    for load in loads:
        load.wait()
    curved = own[...] + prior[...] * d_own[...]
    for k in range(1, nz):
        curved = curved + z_got[k].astype(F32)
    own[...] = curved
    tile = jnp.zeros(small.shape[1:], F32)
    row = lax.broadcasted_iota(jnp.int32, tile.shape, 0)

    def par_sum(slot, values, ss, rs):
        filled = tile
        for i, value in enumerate(values):
            filled = jnp.where(row == i, value, filled)
        small[slot] = filled
        sent = [
            send(small.at[slot], small_got.at[slot, k], ss.at[k], rs.at[k], peer)
            for k, peer in enumerate(par_peers)
        ]
        for copy in sent:
            copy.wait()
        small_got[slot, npar - 1] = filled
        total = tile
        for i in range(npar):
            total = total + small_got[slot, lax.rem(mine - i - 1 + npar, npar)]
        return [total[i : i + 1, :1] for i in range(len(values))]

    along, before = par_sum(
        0, [total_of(d_own[...] * own[...]), total_of(r_own[...] * r_own[...])], s3, r3
    )
    step = before / along
    rounded = (r_own[...] - step * own[...]).astype(BF16)
    out[me] = rounded
    gather = [
        send(out.at[me], out.at[me], s4.at[k], r4.at[k], {"sen": 2 * up[k] + c})
        for k in range(1, nz)
    ]
    gather.append(send(out.at[me], out.at[me], s5.at[0], r5.at[0], sibling))
    kept = rounded.astype(F32)
    (fresh,) = par_sum(1, [total_of(kept * kept)], s7, r7)
    scalars[me] = jnp.where(row == 0, step, jnp.where(row == 1, fresh / before, tile))
    told = [
        send(scalars.at[me], scalars.at[me], s6.at[k], r6.at[k], peer)
        for k, peer in enumerate(sen_peers)
    ]
    passed = []
    for k in range(1, nz):
        gather[k - 1].wait_recv()
        chunk = 2 * down[k] + c
        passed.append(send(out.at[chunk], out.at[chunk], s5.at[k], r5.at[k], sibling))
    for k in range(1, nz):
        gather[k - 1].wait_send()
    gather[-1].wait()
    for copy in passed + told:
        copy.wait()
    for k in order:
        core[k].wait_send()
    for copy in along_z:
        copy.wait_send()


def update(part, direction, residual, prior):
    n, npar = lax.axis_size("sen"), lax.axis_size("par")
    sources, steps, params = part.shape
    if n != sources or npar == 1:
        curved = lax.psum(part, "sen") + prior[None, None, :] * direction
        sums = jnp.stack([direction * curved, residual * residual])
        along, before = lax.psum(jnp.sum(sums, axis=(2, 3)), "par")
        step = before / along
        after = residual - step[:, None, None] * curved
        fresh = lax.psum(jnp.sum(after * after, axis=(1, 2)), "par")
        return after, step[:, None, None], (fresh / before)[:, None, None]
    nz = n // 2
    vm = pl.BlockSpec(memory_space=pltpu.VMEM)
    anywhere = pl.BlockSpec(memory_space=pl.ANY)
    chunk = (steps, params)
    dma = pltpu.SemaphoreType.DMA
    after, scalars = pl.pallas_call(
        functools.partial(update_kernel, n, npar),
        out_shape=(
            jax.ShapeDtypeStruct((sources, steps, params), BF16),
            jax.ShapeDtypeStruct((sources, 8, LANES), F32),
        ),
        in_specs=[vm, anywhere, anywhere, vm],
        out_specs=(vm, vm),
        scratch_shapes=[
            pltpu.VMEM((nz,) + chunk, F32),
            pltpu.VMEM((nz,) + chunk, BF16),
            pltpu.VMEM((nz,) + chunk, BF16),
            pltpu.VMEM(chunk, F32),
            pltpu.VMEM(chunk, F32),
            pltpu.VMEM(chunk, F32),
            pltpu.VMEM((2, 8, LANES), F32),
            pltpu.VMEM((2, npar, 8, LANES), F32),
            dma((2,)),
        ]
        + [dma((nz,))] * 4
        + [dma((npar,))] * 2
        + [dma((nz,))] * 4
        + [dma((n,))] * 2
        + [dma((npar,))] * 2,
        compiler_params=pltpu.CompilerParams(
            collective_id=1, has_side_effects=True, vmem_limit_bytes=32 * 2**20
        ),
        name="update",
    )(part, direction, residual, prior[None, :])
    return after.astype(F32), scalars[:, 0:1, 0:1], scalars[:, 1:2, 0:1]


def on_device(freq_blocks, noise_index, noise_levels, prior, right_side):
    sources, steps, _ = right_side.shape
    freqs = freq_blocks.shape[1]
    consts = [halves(table) for table in tables(steps, freqs)]
    level_ids = jnp.arange(noise_levels.shape[0], dtype=jnp.int32)
    pack = max(1, min(sources, LANES // freq_blocks.shape[2]))
    index = jnp.tile(noise_index.T, (1, pack))
    weights = jnp.sum(
        jnp.where(index[None] == level_ids[:, None, None], noise_levels[:, None, None], F32(0.0)),
        axis=0,
    )
    solution = None
    residual = right_side
    direction = right_side
    for iteration in range(ITERS):
        pred = sum_over_par(forward(consts, freq_blocks, direction))
        part = adjoint(consts, freq_blocks, pred, weights, sources)
        residual, step, ratio = update(part, direction, residual, prior)
        moved = step * direction
        solution = moved if solution is None else solution + moved
        if iteration + 1 < ITERS:
            direction = residual + ratio * direction
    return (solution, residual)


def solution(mesh):
    placed = (P(None, None, "sen", "par"), P("sen", None), P(), P("par"), P(None, None, "par"))
    return jax.shard_map(
        on_device,
        mesh=mesh,
        in_specs=placed,
        out_specs=(P(None, None, "par"), P(None, None, "par")),
        check_vma=False,
    )
```

```python
import functools
import math

import jax
import jax.numpy as jnp
import numpy as np
from jax import lax
from jax.experimental import pallas as pl
from jax.experimental.pallas import tpu as pltpu
from jax.sharding import PartitionSpec as P

ITERS = 2
CHUNKS = 8
AHEAD = 3
UNROLL = 16
LANES = 128
VMEM_BYTES = 58 * 2**20
F32 = jnp.float32
BF16 = jnp.bfloat16
MESH = pl.DeviceIdType.MESH


def tables(steps, freqs):
    period = 2 * steps
    t = np.arange(steps)
    k = np.arange(freqs)
    angle = (k[:, None] * t[None, :] % period) * (2.0 * math.pi / period)
    cos, sin = np.cos(angle), np.sin(angle)
    scale = np.where((k == 0) | (k == period // 2), 1.0, 2.0)[:, None] / period
    rows = lambda a, b: np.stack([a, b], axis=1).reshape(2 * freqs, steps)
    analyse = rows(cos, -sin)
    first = rows(scale * cos, -scale * sin)
    second = rows(-scale * sin, -scale * cos)
    return analyse, first, second


def halves(table):
    high = np.asarray(table, np.float32).astype(jnp.bfloat16)
    low = (np.asarray(table, np.float64) - high.astype(np.float64)).astype(jnp.bfloat16)
    return high, low


def wide(table_high, table_low, x):
    high = x.astype(BF16)
    low = (x - high.astype(F32)).astype(BF16)
    dot = functools.partial(jnp.dot, preferred_element_type=F32)
    return dot(table_high, high) + (dot(table_high, low) + dot(table_low, high))


def chunk_list(freqs):
    edges = [freqs * i // CHUNKS for i in range(CHUNKS + 1)]
    return [(a, b) for a, b in zip(edges[:-1], edges[1:]) if b > a]


def start_copies(blocks, held, sems, chunks):
    copies = []
    for i, (a, b) in enumerate(chunks):
        copy = pltpu.make_async_copy(blocks.at[:, a:b], held.at[:, a:b], sems.at[i])
        copies.append(copy)
    for copy in copies[:AHEAD]:
        copy.start()
    return copies


def forward_kernel(chunks, pack, ah, al, fh, fl, sh, sl, field, blocks, out, held, spec, prod, sems):
    copies = start_copies(blocks, held, sems, chunks)
    sources = field.shape[0]
    rows = ah.shape[0]
    sensors = held.shape[2]
    for b in range(sources):
        made = wide(ah[...], al[...], field[b])
        for j in range(spec.shape[0]):
            spec[j, pl.ds(b, rows, stride=sources), :] = made[:, j * LANES : (j + 1) * LANES]

    def one(k, _):
        at = pl.ds(pl.multiple_of(k * 2 * sources, 2 * sources), 2 * sources)
        lhs = jnp.concatenate([spec[j, at, :].astype(BF16) for j in range(spec.shape[0])], axis=1)
        rhs = jnp.concatenate([held[0, k], held[1, k]], axis=0)
        prod[at, : 2 * sensors] = lax.dot_general(
            lhs, rhs, (((1,), (1,)), ((), ())), preferred_element_type=F32
        )
        return 0

    for i, (a, b) in enumerate(chunks):
        copies[i].wait()
        if i + AHEAD < len(chunks):
            copies[i + AHEAD].start()
        lax.fori_loop(a, b, one, 0, unroll=UNROLL)
    groups = sources // pack
    real, imag = [], []
    for p in range(groups):
        for i in range(pack):
            x = prod[pl.ds(p + i * groups, rows, stride=sources), :]
            real.append(x[:, :sensors])
            imag.append(x[:, sensors : 2 * sensors])
    made = wide(fh[...], fl[...], jnp.concatenate(real, axis=1))
    made = made + wide(sh[...], sl[...], jnp.concatenate(imag, axis=1))
    for p in range(groups):
        out[p] = made[:, p * pack * sensors : (p + 1) * pack * sensors]


def adjoint_kernel(
    chunks, pack, fh, fl, sh, sl, ih, il, pred, weights, blocks, out, held, back, grad, sems
):
    copies = start_copies(blocks, held, sems, chunks)
    sources = out.shape[0]
    rows = fh.shape[0]
    sensors = held.shape[2]
    groups = sources // pack
    weighted = jnp.concatenate([weights[...] * pred[p] for p in range(groups)], axis=1)
    one_part = wide(fh[...], fl[...], weighted)
    two_part = wide(sh[...], sl[...], weighted)
    for p in range(groups):
        for i in range(pack):
            start = (p * pack + i) * sensors
            row = [x[:, start : start + sensors] for x in (one_part, two_part)]
            if 2 * sensors < LANES:
                row.append(jnp.zeros((rows, LANES - 2 * sensors), F32))
            back[pl.ds(p + i * groups, rows, stride=sources), :] = jnp.concatenate(row, axis=1)

    def one(k, _):
        at = pl.ds(pl.multiple_of(k * 2 * sources, 2 * sources), 2 * sources)
        lhs = back[at, : 2 * sensors].astype(BF16)
        rhs = jnp.concatenate([held[0, k], held[1, k]], axis=0)
        made = jnp.dot(lhs, rhs, preferred_element_type=F32)
        for j in range(grad.shape[0]):
            grad[j, at, :] = made[:, j * LANES : (j + 1) * LANES]
        return 0

    for i, (a, b) in enumerate(chunks):
        copies[i].wait()
        if i + AHEAD < len(chunks):
            copies[i + AHEAD].start()
        lax.fori_loop(a, b, one, 0, unroll=UNROLL)
    for b in range(sources):
        x = jnp.concatenate(
            [grad[j, pl.ds(b, rows, stride=sources), :] for j in range(grad.shape[0])], axis=1
        )
        out[b] = wide(ih[...], il[...], x)


def forward(consts, blocks, field):
    (ah, al), (fh, fl), (sh, sl) = consts
    _, freqs, sensors, params = blocks.shape
    sources, steps, _ = field.shape
    pack = max(1, min(sources, 128 // sensors))
    chunks = chunk_list(freqs)
    vm = pl.BlockSpec(memory_space=pltpu.VMEM)
    return pl.pallas_call(
        functools.partial(forward_kernel, chunks, pack),
        out_shape=jax.ShapeDtypeStruct((sources // pack, steps, pack * sensors), F32),
        in_specs=[vm] * 7 + [pl.BlockSpec(memory_space=pl.ANY)],
        out_specs=vm,
        scratch_shapes=[
            pltpu.VMEM(blocks.shape, BF16),
            pltpu.VMEM((params // LANES, 2 * freqs * sources, LANES), F32),
            pltpu.VMEM((2 * freqs * sources, max(LANES, 2 * sensors)), F32),
            pltpu.SemaphoreType.DMA((len(chunks),)),
        ],
        compiler_params=pltpu.CompilerParams(vmem_limit_bytes=VMEM_BYTES),
        name="forward",
    )(ah, al, fh.T, fl.T, sh.T, sl.T, field, blocks)


def adjoint(consts, blocks, pred, weights, sources):
    (ah, al), (fh, fl), (sh, sl) = consts
    _, freqs, sensors, params = blocks.shape
    steps = pred.shape[1]
    pack = sources // pred.shape[0]
    chunks = chunk_list(freqs)
    vm = pl.BlockSpec(memory_space=pltpu.VMEM)
    return pl.pallas_call(
        functools.partial(adjoint_kernel, chunks, pack),
        out_shape=jax.ShapeDtypeStruct((sources, steps, params), F32),
        in_specs=[vm] * 8 + [pl.BlockSpec(memory_space=pl.ANY)],
        out_specs=vm,
        scratch_shapes=[
            pltpu.VMEM(blocks.shape, BF16),
            pltpu.VMEM((2 * freqs * sources, max(LANES, 2 * sensors)), F32),
            pltpu.VMEM((params // LANES, 2 * freqs * sources, LANES), F32),
            pltpu.SemaphoreType.DMA((len(chunks),)),
        ],
        compiler_params=pltpu.CompilerParams(vmem_limit_bytes=VMEM_BYTES),
        name="adjoint",
    )(fh, fl, sh, sl, ah.T, al.T, pred, weights, blocks)


def greet(peers):
    barrier = pltpu.get_barrier_semaphore()
    for peer in peers:
        pl.semaphore_signal(barrier, inc=1, device_id=peer, device_id_type=MESH)
    pl.semaphore_wait(barrier, len(peers))


def send(src, dst, send_sem, recv_sem, peer):
    copy = pltpu.make_async_remote_copy(
        src_ref=src,
        dst_ref=dst,
        send_sem=send_sem,
        recv_sem=recv_sem,
        device_id=peer,
        device_id_type=MESH,
    )
    copy.start()
    return copy


def sum_kernel(n, part, out, got, s1, r1, s2, r2):
    me = lax.axis_index("par")
    others = [lax.rem(me + k, n) for k in range(n)]
    greet([{"par": o} for o in others[1:]])
    first = [
        send(part.at[others[k]], got.at[k], s1.at[k], r1.at[k], {"par": others[k]})
        for k in range(1, n)
    ]
    for copy in first:
        copy.wait_recv()
    total = part[me]
    for k in range(1, n):
        total = total + got[k]
    out[me] = total
    second = [
        send(out.at[me], out.at[me], s2.at[k], r2.at[k], {"par": others[k]}) for k in range(1, n)
    ]
    for copy in first:
        copy.wait_send()
    for copy in second:
        copy.wait()


def sum_over_par(part):
    n = lax.axis_size("par")
    if part.shape[0] != n or n == 1:
        return lax.psum(part, "par")
    vm = pl.BlockSpec(memory_space=pltpu.VMEM)
    return pl.pallas_call(
        functools.partial(sum_kernel, n),
        out_shape=jax.ShapeDtypeStruct(part.shape, part.dtype),
        in_specs=[vm],
        out_specs=vm,
        scratch_shapes=[pltpu.VMEM(part.shape, part.dtype)] + [pltpu.SemaphoreType.DMA((n,))] * 4,
        compiler_params=pltpu.CompilerParams(
            collective_id=0, has_side_effects=True, vmem_limit_bytes=16 * 2**20
        ),
        name="sum_par",
    )(part)


def total_of(x):
    return jnp.sum(jnp.sum(x, axis=0, keepdims=True), axis=1, keepdims=True)


def update_kernel(
    n, npar, part, direction, residual, prior, out, scalars,
    part_own, core_got, staged, z_got, own, d_own, r_own, small, small_got,
    ls, s1, r1, s2, r2, s3, r3, s4, r4, s5, r5, s6, r6, s7, r7,
):
    me = lax.axis_index("sen")
    nz = n // 2
    z, c = me // 2, lax.rem(me, 2)
    sibling = {"sen": 2 * z + 1 - c}
    mine = lax.axis_index("par")
    par_peers = [{"par": lax.rem(mine + k, npar)} for k in range(1, npar)]
    sen_peers = [{"sen": lax.rem(me + k, n)} for k in range(1, n)]
    up = [lax.rem(z + k, nz) for k in range(nz)]
    down = [lax.rem(z + nz - k, nz) for k in range(nz)]
    loads = [
        pltpu.make_async_copy(direction.at[me], d_own, ls.at[0]),
        pltpu.make_async_copy(residual.at[me], r_own, ls.at[1]),
    ]
    order = [k for k in range(1, nz)] + [0]
    mine_in = [
        pltpu.make_async_copy(part.at[2 * up[k] + c], part_own.at[k], ls.at[2 + k])
        for k in range(nz)
    ]
    for load in [mine_in[k] for k in order] + loads:
        load.start()
    greet(sen_peers + par_peers)
    core = {}
    for k in order:
        core[k] = send(part.at[2 * up[k] + 1 - c], core_got.at[k], s1.at[k], r1.at[k], sibling)
    along_z = []
    for k in order:
        mine_in[k].wait()
        core[k].wait_recv()
        summed = part_own[k] + core_got[k]
        if k == 0:
            own[...] = summed
        else:
            staged[k] = summed.astype(BF16)
            along_z.append(
                send(staged.at[k], z_got.at[k], s2.at[k], r2.at[k], {"sen": 2 * up[k] + c})
            )
    for copy in along_z:
        copy.wait_recv()
    for load in loads:
        load.wait()
    curved = own[...] + prior[...] * d_own[...]
    for k in range(1, nz):
        curved = curved + z_got[k].astype(F32)
    own[...] = curved
    tile = jnp.zeros(small.shape[1:], F32)
    row = lax.broadcasted_iota(jnp.int32, tile.shape, 0)

    def par_sum(slot, values, ss, rs):
        filled = tile
        for i, value in enumerate(values):
            filled = jnp.where(row == i, value, filled)
        small[slot] = filled
        sent = [
            send(small.at[slot], small_got.at[slot, k], ss.at[k], rs.at[k], peer)
            for k, peer in enumerate(par_peers)
        ]
        for copy in sent:
            copy.wait()
        small_got[slot, npar - 1] = filled
        total = tile
        for i in range(npar):
            total = total + small_got[slot, lax.rem(mine - i - 1 + npar, npar)]
        return [total[i : i + 1, :1] for i in range(len(values))]

    along, before = par_sum(
        0, [total_of(d_own[...] * own[...]), total_of(r_own[...] * r_own[...])], s3, r3
    )
    step = before / along
    rounded = (r_own[...] - step * own[...]).astype(BF16)
    out[me] = rounded
    gather = [
        send(out.at[me], out.at[me], s4.at[k], r4.at[k], {"sen": 2 * up[k] + c})
        for k in range(1, nz)
    ]
    gather.append(send(out.at[me], out.at[me], s5.at[0], r5.at[0], sibling))
    kept = rounded.astype(F32)
    (fresh,) = par_sum(1, [total_of(kept * kept)], s7, r7)
    scalars[me] = jnp.where(row == 0, step, jnp.where(row == 1, fresh / before, tile))
    told = [
        send(scalars.at[me], scalars.at[me], s6.at[k], r6.at[k], peer)
        for k, peer in enumerate(sen_peers)
    ]
    passed = []
    for k in range(1, nz):
        gather[k - 1].wait_recv()
        chunk = 2 * down[k] + c
        passed.append(send(out.at[chunk], out.at[chunk], s5.at[k], r5.at[k], sibling))
    for k in range(1, nz):
        gather[k - 1].wait_send()
    gather[-1].wait()
    for copy in passed + told:
        copy.wait()
    for k in order:
        core[k].wait_send()
    for copy in along_z:
        copy.wait_send()


def update(part, direction, residual, prior):
    n, npar = lax.axis_size("sen"), lax.axis_size("par")
    sources, steps, params = part.shape
    if n != sources or npar == 1:
        curved = lax.psum(part, "sen") + prior[None, None, :] * direction
        sums = jnp.stack([direction * curved, residual * residual])
        along, before = lax.psum(jnp.sum(sums, axis=(2, 3)), "par")
        step = before / along
        after = residual - step[:, None, None] * curved
        fresh = lax.psum(jnp.sum(after * after, axis=(1, 2)), "par")
        return after, step[:, None, None], (fresh / before)[:, None, None]
    nz = n // 2
    vm = pl.BlockSpec(memory_space=pltpu.VMEM)
    anywhere = pl.BlockSpec(memory_space=pl.ANY)
    chunk = (steps, params)
    dma = pltpu.SemaphoreType.DMA
    after, scalars = pl.pallas_call(
        functools.partial(update_kernel, n, npar),
        out_shape=(
            jax.ShapeDtypeStruct((sources, steps, params), BF16),
            jax.ShapeDtypeStruct((sources, 8, LANES), F32),
        ),
        in_specs=[anywhere, anywhere, anywhere, vm],
        out_specs=(vm, vm),
        scratch_shapes=[
            pltpu.VMEM((nz,) + chunk, F32),
            pltpu.VMEM((nz,) + chunk, F32),
            pltpu.VMEM((nz,) + chunk, BF16),
            pltpu.VMEM((nz,) + chunk, BF16),
            pltpu.VMEM(chunk, F32),
            pltpu.VMEM(chunk, F32),
            pltpu.VMEM(chunk, F32),
            pltpu.VMEM((2, 8, LANES), F32),
            pltpu.VMEM((2, npar, 8, LANES), F32),
            dma((2 + nz,)),
        ]
        + [dma((nz,))] * 4
        + [dma((npar,))] * 2
        + [dma((nz,))] * 4
        + [dma((n,))] * 2
        + [dma((npar,))] * 2,
        compiler_params=pltpu.CompilerParams(
            collective_id=1, has_side_effects=True, vmem_limit_bytes=32 * 2**20
        ),
        name="update",
    )(part, direction, residual, prior[None, :])
    return after.astype(F32), scalars[:, 0:1, 0:1], scalars[:, 1:2, 0:1]


def on_device(freq_blocks, noise_index, noise_levels, prior, right_side):
    sources, steps, _ = right_side.shape
    freqs = freq_blocks.shape[1]
    consts = [halves(table) for table in tables(steps, freqs)]
    level_ids = jnp.arange(noise_levels.shape[0], dtype=jnp.int32)
    pack = max(1, min(sources, LANES // freq_blocks.shape[2]))
    index = jnp.tile(noise_index.T, (1, pack))
    weights = jnp.sum(
        jnp.where(index[None] == level_ids[:, None, None], noise_levels[:, None, None], F32(0.0)),
        axis=0,
    )
    solution = None
    residual = right_side
    direction = right_side
    for iteration in range(ITERS):
        pred = sum_over_par(forward(consts, freq_blocks, direction))
        part = adjoint(consts, freq_blocks, pred, weights, sources)
        residual, step, ratio = update(part, direction, residual, prior)
        moved = step * direction
        solution = moved if solution is None else solution + moved
        if iteration + 1 < ITERS:
            direction = residual + ratio * direction
    return (solution, residual)


def solution(mesh):
    placed = (P(None, None, "sen", "par"), P("sen", None), P(), P("par"), P(None, None, "par"))
    return jax.shard_map(
        on_device,
        mesh=mesh,
        in_specs=placed,
        out_specs=(P(None, None, "par"), P(None, None, "par")),
        check_vma=False,
    )
```
